256 devices in a mesh: rep: 64 (over x, y_hi, z), fsdp: 4 (over y_lo, core).
Axes of the slice: x: 4, y: 4 (y_hi: 2, y_lo: 2; y = y_hi * 2 + y_lo), z: 8, core: 2. Of those that a mesh axis runs over, the one named last changes fastest.
Arguments:
- hidden: bfloat16 [64, 1024, 4608], P('rep', 'fsdp'), may hold values from -6 to 6
- upstream: bfloat16 [64, 1024, 1024], P('rep', 'fsdp'), may hold values from -6 to 6
- weights: bfloat16 [64, 4608, 1024], P('rep', 'fsdp'), may hold values from -16 to 16
- moment_one: bfloat16 [64, 4608, 1024], P('rep', 'fsdp'), may hold values from -0.59765625 to 0.59765625
- moment_two: bfloat16 [64, 4608, 1024], P('rep', 'fsdp'), may hold values from 0.0029907227 to 0.099609375
- global_params: float32 [4, 1152, 1024], P('fsdp', 'rep'), may hold values from -6 to 6
- outer_momentum: float32 [4, 1152, 1024], P('fsdp', 'rep'), may hold values from -2 to 2
Outputs:
- values: bfloat16 [64, 1024, 1024], P('rep', 'fsdp')
- merged: bfloat16 [64, 4608, 1024], P('rep', 'fsdp')
- new_global: float32 [4, 1152, 1024], P('fsdp', 'rep')
- new_momentum: float32 [4, 1152, 1024], P('fsdp', 'rep')
The draws below stay inside these ranges and needn't reach their ends.
All inputs are finite; a program needn't handle non-finite values.
Results may differ from the reference program's by a relative error of at most 0.007.
Values may be sent and summed in bfloat16 or wider, within the bound.
No kernel may reach another device: no remote copies, remote signals or barrier semaphores. Data moves between devices by JAX's collectives and lax.ppermute only.
A program may use at most 128 MiB of HBM per device.

```python
import math
import jax
import jax.numpy as jnp
from jax import lax

D = 4608
TOK_DEV = 256
COLS = 1024
RTOK = 1024
REPLICAS = 64
SHARDS = 4
FSDP_ROWS = 1152


def strengthened(result, own_key, source, target, blocks, factor):
    def block_of(axis_at):
        return (jnp.arange(result.shape[axis_at]) // (result.shape[axis_at] // blocks)).reshape((-1,) + (1,) * (result.ndim - 1 - axis_at))

    first = jax.random.permutation(own_key, blocks)[block_of(target)]
    second = (block_of(target) + blocks // 2) % blocks
    return jnp.where((block_of(source) == first) | (block_of(source) == second), factor * result, result)


def levels(stream_key, extent, shards, low, high):
    def one(dim, shards_of):
        steps = jax.random.uniform(jax.random.fold_in(jax.random.fold_in(stream_key, 6), dim), (shards_of,), jnp.float32, low / len(shards), high / len(shards))
        return jnp.repeat(jnp.exp(steps), extent[dim] // shards_of).reshape((-1,) + (1,) * (len(extent) - dim - 1))

    gain = one(*shards[0])
    for cut in shards[1:]:
        gain = gain * one(*cut)
    return gain


def noise(stream_key, dims, width, most, pieces=(), kind=jnp.bfloat16):
    result = jax.random.normal(stream_key, dims, jnp.float32) * width
    if len(pieces) > 0:
        result = levels(stream_key, dims, pieces, -0.22, 0.18) * result
    return jnp.clip(result, min=-most, max=most).astype(kind)


def noise_with(key, extent, width, bound, pieces, heavy, held_as=jnp.bfloat16):
    entries = width * jax.random.normal(key, extent, jnp.float32)
    if pieces:
        entries = entries * levels(key, extent, pieces, -0.22, 0.18)
    return jnp.clip(strengthened(entries, jax.random.fold_in(key, 3), *heavy), -bound, bound).astype(held_as)


def setup_inputs(seed: int = 0) -> dict:
    seeds = jax.random.split(jax.random.key(seed), 8)
    hidden = noise(seeds[0], (REPLICAS, RTOK, D), 1.0, 6.0, ((0, 64), (1, 4)))
    upstream = noise(seeds[1], (REPLICAS, RTOK, COLS), 1.0, 6.0, ((0, 64), (1, 4)))
    weights = noise_with(seeds[2], (REPLICAS, D, COLS), 1.0, 16.0, ((0, 64), (1, 4)), (0, 1, 64, 4.0))
    moment_one = noise(seeds[3], (REPLICAS, D, COLS), 0.1, 0.59765625, ((0, 64), (1, 4)))
    moment_two = jnp.clip(jnp.exp(math.log(0.099609375) - 3.5057412 * jax.random.uniform(seeds[4], (REPLICAS, D, COLS), jnp.float32) ** levels(seeds[4], (REPLICAS, D, COLS), ((0, 64), (1, 4)), -0.2, 0.2)), 0.0029907227, 0.099609375).astype(jnp.bfloat16)
    global_params = noise(seeds[5], (SHARDS, FSDP_ROWS, COLS), 1.0, 6.0, ((0, 4), (1, 64)), jnp.float32)
    outer_momentum = noise(seeds[6], (SHARDS, FSDP_ROWS, COLS), 0.3, 2.0, ((0, 4), (1, 64)), jnp.float32)
    return {"hidden": hidden, "upstream": upstream, "weights": weights, "moment_one": moment_one, "moment_two": moment_two, "global_params": global_params, "outer_momentum": outer_momentum}


beta_one = 0.9
beta_two = 0.95
bias_one = 1.0 - 0.9 ** 8
bias_two = 1.0 - 0.95 ** 8
inner_rate = 0.25
decay_rate = 0.1
epsilon = 1e-08
outer_rate = 0.7
outer_mu = 0.9
mixing = 0.5

def reference(hidden, upstream, weights, moment_one, moment_two, global_params, outer_momentum):
    factor = float(D) ** (-0.5)
    summed = lax.optimization_barrier(jnp.sum(weights, axis=0, dtype=jnp.float32))
    global_now = global_params.reshape(D, COLS)
    pseudo = global_now - summed / REPLICAS
    momentum = outer_mu * outer_momentum.reshape(D, COLS) + pseudo
    renewed = global_now - outer_rate * (pseudo + outer_mu * momentum)

    def per_replica(member):
        rows_in, grads_in, current_w, first_in, second_in = member
        outputs = (jnp.dot(rows_in, current_w, preferred_element_type=jnp.float32) * factor).astype(jnp.bfloat16)
        blocks_in = rows_in.reshape(SHARDS, TOK_DEV, D)
        blocks_grad = grads_in.reshape(SHARDS, TOK_DEV, COLS)
        gradient = jnp.zeros((D, COLS), jnp.float32)
        for position in range(SHARDS):
            partial_term = lax.dot_general(blocks_in[position], blocks_grad[position], (((0,), (0,)), ((), ())), preferred_element_type=jnp.float32) * factor
            rounded = lax.optimization_barrier(partial_term.astype(jnp.bfloat16))
            gradient = gradient + rounded.astype(jnp.float32)
        moment_new = beta_one * first_in.astype(jnp.float32) + (1.0 - beta_one) * gradient
        second_new = beta_two * second_in.astype(jnp.float32) + (1.0 - beta_two) * gradient * gradient
        stepped = moment_new / bias_one / (jnp.sqrt(second_new / bias_two) + epsilon)
        current = current_w.astype(jnp.float32)
        updated = current - inner_rate * (stepped + decay_rate * current)
        mixed = (mixing * updated + (1.0 - mixing) * renewed).astype(jnp.bfloat16)
        return (outputs, mixed)
    values, merged = lax.map(per_replica, (hidden, upstream, weights, moment_one, moment_two))
    return (values, merged, renewed.reshape(SHARDS, FSDP_ROWS, COLS), momentum.reshape(SHARDS, FSDP_ROWS, COLS))
```

```python
import jax
import jax.numpy as jnp
from jax import lax
from jax.sharding import PartitionSpec as P

beta_one = 0.9
beta_two = 0.95
bias_one = 1.0 - 0.9**8
bias_two = 1.0 - 0.95**8
inner_rate = 0.25
decay_rate = 0.1
epsilon = 1e-08
outer_rate = 0.7
outer_mu = 0.9
mixing = 0.5

NX, NYH, NZ = 4, 2, 8
NYL, NC = 2, 2
BOTH = ("rep", "fsdp")
X_GROUPS = [[(x * NYH + h) * NZ + z for x in range(NX)] for h in range(NYH) for z in range(NZ)]
Z_GROUPS = [[(x * NYH + h) * NZ + z for z in range(NZ)] for x in range(NX) for h in range(NYH)]


def pairs(move):
    found = []
    for x in range(NX):
        for h in range(NYH):
            for z in range(NZ):
                for y in range(NYL):
                    for c in range(NC):
                        h2, y2, c2 = move(h, y, c)
                        found.append(
                            (
                                ((x * NYH + h) * NZ + z) * 4 + y * 2 + c,
                                ((x * NYH + h2) * NZ + z) * 4 + y2 * 2 + c2,
                            )
                        )
    return found


TO_OTHER_CORE = pairs(lambda h, y, c: (h, y, 1 - c))
TO_OTHER_CHIP = pairs(lambda h, y, c: (h, 1 - y, c))
TO_OTHER_HALF = pairs(lambda h, y, c: (1 - h, y, c))


def over_x(array):
    return lax.all_to_all(array, "rep", 0, 0, axis_index_groups=X_GROUPS)


def over_z(array):
    return lax.all_to_all(array, "rep", 0, 0, axis_index_groups=Z_GROUPS)


def swap(array, to):
    return lax.ppermute(array, BOTH, to)


def dot(a, b, contract=((1,), (0,))):
    return lax.dot_general(a, b, (contract, ((), ())), preferred_element_type=jnp.float32)


def on_device(hidden, upstream, weights, moment_one, moment_two, global_params, outer_momentum):
    bf16, f32 = jnp.bfloat16, jnp.float32
    tokens, width = hidden.shape[1:]
    rows, cols = weights.shape[1:]
    factor = float(width) ** (-0.5)
    own_rows = global_params.shape[1]
    block = rows // NX
    lane = cols // NZ
    half = block // NYH
    chip = width // NYL
    rep, fsdp = lax.axis_index("rep"), lax.axis_index("fsdp")
    core, pair = fsdp % NC, fsdp // NC
    side = (rep // NZ) % NYH

    w = weights[0]
    h = hidden[0]
    u = upstream[0]

    parts_x = over_x(w.reshape(NX, block, cols))

    h_sent = lax.dynamic_slice_in_dim(h, (1 - pair) * chip, chip, 1)
    h_kept = lax.dynamic_slice_in_dim(h, pair * chip, chip, 1)
    h_got = swap(h_sent, TO_OTHER_CHIP)
    u_got = swap(u, TO_OTHER_CHIP)
    w_other = swap(w, TO_OTHER_CORE)

    state = jnp.stack([global_params[0], outer_momentum[0]]).reshape(2, own_rows, NZ, lane)
    state = over_z(state.transpose(2, 0, 1, 3))
    state = state.transpose(1, 0, 2, 3).reshape(2, half, lane)
    state_far = swap(state, TO_OTHER_HALF)
    first = jnp.where(side == 0, state, state_far)
    second = jnp.where(side == 0, state_far, state)
    state = jnp.concatenate([first, second], axis=1)

    sum_x = jnp.sum(parts_x.astype(f32), axis=0).astype(bf16)
    parts_z = over_z(sum_x.reshape(block, NZ, lane).transpose(1, 0, 2))
    sum_z = jnp.sum(parts_z.astype(f32), axis=0)
    summed = sum_z + swap(sum_z.astype(bf16), TO_OTHER_HALF).astype(f32)
    pseudo = state[0] - summed / lax.axis_size("rep")
    momentum = outer_mu * state[1] + pseudo
    renewed = (state[0] - outer_rate * (pseudo + outer_mu * momentum)).astype(bf16)

    owned = lax.dynamic_slice_in_dim(summed, side * half, half, 0).astype(bf16)
    owned = jnp.pad(owned.reshape(NZ, own_rows, lane), ((0, 0), (0, 32 - own_rows), (0, 0)))
    spread_z = over_z(
        jnp.concatenate([jnp.broadcast_to(renewed, (NZ, block, lane)), owned], axis=1)
    )
    spread = over_x(jnp.broadcast_to(spread_z[:, :block], (NX, NZ, block, lane)))
    spread = spread.transpose(0, 2, 1, 3).reshape(rows, cols)

    owned = spread_z[:, block : block + own_rows].transpose(1, 0, 2).reshape(own_rows, cols)
    pseudo = global_params[0] - owned.astype(f32) / lax.axis_size("rep")
    new_momentum = outer_mu * outer_momentum[0] + pseudo
    new_global = global_params[0] - outer_rate * (pseudo + outer_mu * new_momentum)

    def project(part):
        mine = lax.dynamic_slice_in_dim(part, core * rows, rows, 1)
        theirs = lax.dynamic_slice_in_dim(part, (1 - core) * rows, rows, 1)
        return (dot(mine, w) + dot(theirs, w_other)) * factor

    far = swap(project(h_got).astype(bf16), TO_OTHER_CHIP)
    values = (project(h_kept) + far.astype(f32)).astype(bf16)

    def mine_of(part):
        return lax.dynamic_slice_in_dim(part, core * rows, rows, 1)

    def theirs_of(part):
        return lax.dynamic_slice_in_dim(part, (1 - core) * rows, rows, 1)

    near_other = swap(theirs_of(h_kept), TO_OTHER_CORE)
    u_other = swap(u, TO_OTHER_CORE)
    far_other = swap(theirs_of(h_got), TO_OTHER_CORE)
    u_far_other = swap(u_got, TO_OTHER_CORE)
    t = ((0,), (0,))
    gradient = dot(mine_of(h_kept), u, t) + dot(near_other, u_other, t)
    gradient = gradient + dot(mine_of(h_got), u_got, t) + dot(far_other, u_far_other, t)
    gradient = gradient * factor

    moment_new = beta_one * moment_one[0].astype(f32) + (1.0 - beta_one) * gradient
    second_new = beta_two * moment_two[0].astype(f32) + (1.0 - beta_two) * gradient * gradient
    stepped = moment_new / bias_one / (jnp.sqrt(second_new / bias_two) + epsilon)
    current = w.astype(f32)
    updated = current - inner_rate * (stepped + decay_rate * current)
    merged = (mixing * updated + (1.0 - mixing) * spread.astype(f32)).astype(bf16)
    return (values[None], merged[None], new_global[None], new_momentum[None])


def solution(mesh):
    return jax.shard_map(
        on_device,
        mesh=mesh,
        in_specs=(
            P("rep", "fsdp", None),
            P("rep", "fsdp", None),
            P("rep", "fsdp", None),
            P("rep", "fsdp", None),
            P("rep", "fsdp", None),
            P("fsdp", "rep", None),
            P("fsdp", "rep", None),
        ),
        out_specs=(
            P("rep", "fsdp", None),
            P("rep", "fsdp", None),
            P("fsdp", "rep", None),
            P("fsdp", "rep", None),
        ),
        check_vma=False,
    )
```

```python
import jax
import jax.numpy as jnp
from jax import lax
from jax.experimental import pallas as pl
from jax.experimental.pallas import tpu as pltpu
from jax.sharding import PartitionSpec as P

beta_one = 0.9
beta_two = 0.95
bias_one = 1.0 - 0.9**8
bias_two = 1.0 - 0.95**8
inner_rate = 0.25
decay_rate = 0.1
epsilon = 1e-08
outer_rate = 0.7
outer_mu = 0.9
mixing = 0.5

NX, NYH, NZ = 4, 2, 8
NYL, NC = 2, 2
BOTH = ("rep", "fsdp")
PLANE = NYH * NZ
HZ_GROUPS = [[x * PLANE + k for k in range(PLANE)] for x in range(NX)]
Z_GROUPS = [[(x * NYH + h) * NZ + z for z in range(NZ)] for x in range(NX) for h in range(NYH)]


def pairs(move):
    found = []
    for x in range(NX):
        for h in range(NYH):
            for z in range(NZ):
                for y in range(NYL):
                    for c in range(NC):
                        x2, y2, c2 = move(x, y, c)
                        found.append(
                            (
                                ((x * NYH + h) * NZ + z) * 4 + y * 2 + c,
                                ((x2 * NYH + h) * NZ + z) * 4 + y2 * 2 + c2,
                            )
                        )
    return found


TO_OTHER_CORE = pairs(lambda x, y, c: (x, y, 1 - c))
TO_OTHER_CHIP = pairs(lambda x, y, c: (x, 1 - y, c))
TO_X = [pairs(lambda x, y, c, d=d: ((x + d) % NX, y, c)) for d in range(NX)]

MIB = 1024 * 1024
BF16, F32 = jnp.bfloat16, jnp.float32


def over(array, groups):
    return lax.all_to_all(array, "rep", 0, 0, axis_index_groups=groups)


def swap(array, to):
    return lax.ppermute(array, BOTH, to)


def dot(a, b):
    return jnp.dot(a, b, preferred_element_type=F32)


def dot_t(a, b):
    return lax.dot_general(a, b, (((0,), (0,)), ((), ())), preferred_element_type=F32)


def inside(array):
    return pltpu.with_memory_space_constraint(array, pltpu.VMEM)


def outside(array):
    return pltpu.with_memory_space_constraint(array, pltpu.HBM)


def call(kernel, grid, in_specs, out_specs, out_shape, flops, moved, at, *operands):
    spec = pltpu.PrefetchScalarGridSpec(
        num_scalar_prefetch=1, grid=grid, in_specs=in_specs, out_specs=out_specs
    )
    return pl.pallas_call(
        kernel,
        grid_spec=spec,
        out_shape=out_shape,
        compiler_params=pltpu.CompilerParams(vmem_limit_bytes=48 * MIB),
        cost_estimate=pl.CostEstimate(flops=flops, bytes_accessed=moved, transcendentals=0),
    )(at, *operands)


def copy_out(places, array, shapes, at, after=()):
    count = len(shapes)

    def kernel(at_ref, x_ref, *rest):
        outs = rest[len(after) : len(after) + count]
        *held, in_sems, out_sems = rest[len(after) + count :]
        ins = [
            pltpu.make_async_copy(x_ref.at[place], held[k], in_sems.at[k])
            for k, place in enumerate(places(at_ref))
        ]
        backs = [pltpu.make_async_copy(held[k], outs[k], out_sems.at[k]) for k in range(count)]
        for copy in ins:
            copy.start()
        for copy, back in zip(ins, backs, strict=True):
            copy.wait()
            back.start()
        for back in backs:
            back.wait()

    hbm = pl.BlockSpec(memory_space=pl.ANY)
    size = sum(x[0] * x[1] for x in shapes)
    return pl.pallas_call(
        kernel,
        in_specs=[pl.BlockSpec(memory_space=pltpu.SMEM), hbm] + [hbm] * len(after),
        out_specs=[hbm] * count,
        out_shape=[pltpu.HBM(x, BF16) for x in shapes],
        scratch_shapes=[pltpu.VMEM(x, BF16) for x in shapes]
        + [pltpu.SemaphoreType.DMA((count,)), pltpu.SemaphoreType.DMA((count,))],
        compiler_params=pltpu.CompilerParams(vmem_limit_bytes=8 * MIB),
        cost_estimate=pl.CostEstimate(flops=0, bytes_accessed=4 * size, transcendentals=0),
    )(at, outside(array), *after)


def cut_weights(at, w):
    block = w.shape[0] // NX

    def places(at_ref):
        bases = [lax.rem(at_ref[0] + d, NX) * block for d in range(1, NX)]
        return [(pl.ds(pl.multiple_of(base, 16), block), slice(None)) for base in bases]

    return copy_out(places, w, [(block, w.shape[1])] * (NX - 1), at)


def cut_hidden(at, h, after):
    toks, width = h.shape
    chip, rows = width // NYL, width // (NYL * NC)

    def places(at_ref):
        far, near = (1 - at_ref[5]) * chip, at_ref[3] * rows
        return [
            (slice(None), pl.ds(pl.multiple_of(far, 128), chip)),
            (slice(None), pl.ds(pl.multiple_of(near, 128), rows)),
        ]

    return copy_out(places, h, [(toks, chip), (toks, rows)], at, [after])


def sum_over_x(blocks, after):
    block, cols = blocks[0].shape
    half, lane = block // NYH, cols // NZ

    def kernel(w_ref, a_ref, b_ref, c_ref, after_ref, o_ref, held, sems):
        copies = []
        for i in range(NYH):
            rows = pl.ds(i * half, half)
            for z in range(NZ):
                at_z = (rows, pl.ds(z * lane, lane))
                total = w_ref[at_z].astype(F32) + a_ref[at_z].astype(F32)
                total = total + (b_ref[at_z].astype(F32) + c_ref[at_z].astype(F32))
                held[i, z] = total.astype(BF16)
            copies.append(pltpu.make_async_copy(held.at[i], o_ref.at[i], sems.at[i]))
            copies[-1].start()
        for copy in copies:
            copy.wait()

    shape = (NYH, NZ, half, lane)
    return pl.pallas_call(
        kernel,
        in_specs=[pl.BlockSpec(memory_space=pltpu.VMEM)] * NX + [pl.BlockSpec(memory_space=pl.ANY)],
        out_specs=pl.BlockSpec(memory_space=pl.ANY),
        out_shape=pltpu.HBM(shape, BF16),
        scratch_shapes=[pltpu.VMEM(shape, BF16), pltpu.SemaphoreType.DMA((NYH,))],
        compiler_params=pltpu.CompilerParams(vmem_limit_bytes=8 * MIB),
        cost_estimate=pl.CostEstimate(flops=3 * block * cols, bytes_accessed=10 * block * cols, transcendentals=0),
    )(*[inside(x) for x in blocks], after)


def outer_step(parts, state, replicas, *after):
    plane = parts.shape[0]

    def kernel(p_ref, s_ref, *rest):
        r_ref, o_ref, held, sems = rest[-4:]
        summed = p_ref[0].astype(F32)
        for k in range(1, plane):
            summed = summed + p_ref[k].astype(F32)
        pseudo = s_ref[0] - summed / replicas
        momentum = outer_mu * s_ref[1] + pseudo
        renewed = s_ref[0] - outer_rate * (pseudo + outer_mu * momentum)
        held[...] = renewed.astype(BF16)
        copies = [pltpu.make_async_copy(held, r_ref.at[k], sems.at[k]) for k in range(plane)]
        for copy in copies:
            copy.start()
        o_ref[0] = renewed
        o_ref[1] = momentum
        for copy in copies:
            copy.wait()

    vmem = pl.BlockSpec(memory_space=pltpu.VMEM)
    hbm = pl.BlockSpec(memory_space=pl.ANY)
    return pl.pallas_call(
        kernel,
        in_specs=[vmem, vmem] + [hbm] * len(after),
        out_specs=[hbm, vmem],
        out_shape=[pltpu.HBM(parts.shape, BF16), pltpu.HBM(state.shape, F32)],
        scratch_shapes=[pltpu.VMEM(parts.shape[1:], BF16), pltpu.SemaphoreType.DMA((plane,))],
        compiler_params=pltpu.CompilerParams(vmem_limit_bytes=8 * MIB),
        cost_estimate=pl.CostEstimate(flops=2 * parts.size, bytes_accessed=4 * parts.size, transcendentals=0),
    )(inside(parts), inside(state), *after)


def project(at, got, hidden, w, w_other, factor, after):
    rows, cols = w.shape
    toks = got.shape[0]
    steps = 4
    wide = cols // steps

    def kernel(at_ref, a_ref, b_ref, c_ref, d_ref, w_ref, v_ref, after_ref, far_ref, near_ref):
        far_ref[...] = ((dot(a_ref[...], w_ref[...]) + dot(b_ref[...], v_ref[...])) * factor).astype(BF16)
        near_ref[...] = (dot(c_ref[...], w_ref[...]) + dot(d_ref[...], v_ref[...])) * factor

    def left(k):
        return pl.BlockSpec((toks, rows), lambda i, at: (0, at[k]))

    column = pl.BlockSpec((toks, wide), lambda i, at: (0, i))
    wspec = pl.BlockSpec((rows, wide), lambda i, at: (0, i))
    return call(
        kernel,
        (steps,),
        [left(2), left(4), left(1), left(3), wspec, wspec, pl.BlockSpec(memory_space=pl.ANY)],
        [column, column],
        [jax.ShapeDtypeStruct((toks, cols), BF16), jax.ShapeDtypeStruct((toks, cols), F32)],
        8 * toks * rows * cols,
        4 * rows * cols + 8 * toks * rows,
        at,
        got,
        got,
        outside(hidden),
        outside(hidden),
        outside(w),
        outside(w_other),
        after,
    )


def hold(array, *after):
    hbm = pl.BlockSpec(memory_space=pl.ANY)
    return pl.pallas_call(
        lambda *refs: None,
        in_specs=[hbm] * (1 + len(after)),
        out_specs=hbm,
        out_shape=jax.ShapeDtypeStruct(array.shape, array.dtype),
        input_output_aliases={0: 0},
        compiler_params=pltpu.CompilerParams(vmem_limit_bytes=MIB),
    )(array, *after)


def finish(near, far, outer):
    def kernel(n_ref, f_ref, outer_ref, o_ref, out_ref):
        o_ref[...] = (n_ref[...] + f_ref[...].astype(F32)).astype(BF16)

    vmem, hbm = pl.BlockSpec(memory_space=pltpu.VMEM), pl.BlockSpec(memory_space=pl.ANY)
    return pl.pallas_call(
        kernel,
        in_specs=[vmem, vmem, hbm],
        out_specs=[vmem, hbm],
        out_shape=[jax.ShapeDtypeStruct(near.shape, BF16), pltpu.HBM(outer.shape, F32)],
        input_output_aliases={2: 1},
        compiler_params=pltpu.CompilerParams(vmem_limit_bytes=16 * MIB),
        cost_estimate=pl.CostEstimate(flops=near.size, bytes_accessed=8 * near.size, transcendentals=0),
    )(near, far, outside(outer))


def inner_step(at, hidden, near, far_got, far, upstreams, w, m1, m2, factor, after):
    rows, cols = w.shape
    toks = hidden.shape[0]
    tall = 384
    steps = rows // tall

    def kernel(at_ref, h_ref, n_ref, g_ref, f_ref, hu_ref, nu_ref, gu_ref, fu_ref, w_ref, m1_ref, m2_ref, after_ref, o_ref):
        gradient = dot_t(h_ref[...], hu_ref[...]) + dot_t(n_ref[...], nu_ref[...])
        gradient = gradient + dot_t(g_ref[...], gu_ref[...]) + dot_t(f_ref[...], fu_ref[...])
        gradient = gradient * factor
        moment_new = beta_one * m1_ref[...].astype(F32) + (1.0 - beta_one) * gradient
        second_new = beta_two * m2_ref[...].astype(F32) + (1.0 - beta_two) * gradient * gradient
        scale = jnp.sqrt(second_new * (1.0 / bias_two)) + epsilon
        stepped = moment_new * (mixing * inner_rate / bias_one) / scale
        o_ref[...] = (mixing * (1.0 - inner_rate * decay_rate)) * w_ref[...].astype(F32) - stepped

    def left(first):
        return pl.BlockSpec((toks, tall), first)

    whole = pl.BlockSpec((toks, cols), lambda i, at: (0, 0))
    own = pl.BlockSpec((tall, cols), lambda i, at: (i, 0))
    spec = pltpu.PrefetchScalarGridSpec(
        num_scalar_prefetch=1,
        grid=(steps,),
        in_specs=[
            left(lambda i, at: (0, at[1] * steps + i)),
            left(lambda i, at: (0, i)),
            left(lambda i, at: (0, at[2] * steps + i)),
            left(lambda i, at: (0, i)),
            whole,
            whole,
            whole,
            whole,
            own,
            own,
            own,
            pl.BlockSpec(memory_space=pl.ANY),
        ],
        out_specs=own,
    )
    operands = [outside(hidden), near, far_got, far] + upstreams + [outside(w), outside(m1), outside(m2), after]
    return pl.pallas_call(
        kernel,
        grid_spec=spec,
        out_shape=pltpu.HBM((rows, cols), F32),
        compiler_params=pltpu.CompilerParams(vmem_limit_bytes=40 * MIB),
        cost_estimate=pl.CostEstimate(
            flops=8 * toks * rows * cols, bytes_accessed=10 * rows * cols, transcendentals=0
        ),
    )(at, *operands)


def merge(at, kept, spread):
    rows, cols = kept.shape
    plane, half, lane = spread[0].shape
    nz = plane // NYH
    block = NYH * half

    def kernel(at_ref, k_ref, a_ref, b_ref, c_ref, d_ref, o_ref, kept_ref, held, in_sems, out_sems):
        refs = [a_ref, b_ref, c_ref, d_ref]
        places = [pl.ds(pl.multiple_of(lax.rem(at_ref[0] + NX - d, NX) * block, 16), block) for d in range(NX)]
        ins = [pltpu.make_async_copy(k_ref.at[places[d]], kept_ref.at[d], in_sems.at[d]) for d in range(NX)]
        outs = [pltpu.make_async_copy(held.at[d], o_ref.at[places[d]], out_sems.at[d]) for d in range(NX)]
        for copy in ins:
            copy.start()
        for d in range(NX):
            ins[d].wait()
            for i in range(NYH):
                for z in range(nz):
                    at_z = (d, pl.ds(i * half, half), pl.ds(z * lane, lane))
                    new = (1.0 - mixing) * refs[d][i * nz + z].astype(F32)
                    held[at_z] = (kept_ref[at_z] + new).astype(BF16)
            outs[d].start()
        for copy in outs:
            copy.wait()

    vmem, hbm = pl.BlockSpec(memory_space=pltpu.VMEM), pl.BlockSpec(memory_space=pl.ANY)
    return pl.pallas_call(
        kernel,
        in_specs=[pl.BlockSpec(memory_space=pltpu.SMEM), hbm] + [vmem] * NX,
        out_specs=hbm,
        out_shape=jax.ShapeDtypeStruct((rows, cols), BF16),
        scratch_shapes=[
            pltpu.VMEM((NX, block, cols), F32),
            pltpu.VMEM((NX, block, cols), BF16),
            pltpu.SemaphoreType.DMA((NX,)),
            pltpu.SemaphoreType.DMA((NX,)),
        ],
        compiler_params=pltpu.CompilerParams(vmem_limit_bytes=24 * MIB),
        cost_estimate=pl.CostEstimate(flops=2 * rows * cols, bytes_accessed=8 * rows * cols, transcendentals=0),
    )(at, outside(kept), *[inside(x) for x in spread])


def on_device(hidden, upstream, weights, moment_one, moment_two, global_params, outer_momentum):
    width = hidden.shape[2]
    rows, cols = weights.shape[1:]
    factor = float(width) ** (-0.5)
    own_rows = global_params.shape[1]
    block = rows // NX
    lane = cols // NZ
    half = block // NYH
    rep, fsdp = lax.axis_index("rep"), lax.axis_index("fsdp")
    core, pair = fsdp % NC, fsdp // NC
    x_at = rep // PLANE
    sibling = pair * NC + 1 - core
    at = jnp.stack([x_at, fsdp, core, sibling, 1 - core, pair]).astype(jnp.int32)

    w, h, u = weights[0], hidden[0], upstream[0]

    sent = cut_weights(at, w)
    got = [swap(x, TO_X[d]) for d, x in enumerate(sent, 1)]

    h_sent, h_near = cut_hidden(at, h, sent[0])
    h_got = swap(h_sent, TO_OTHER_CHIP)
    u_got = swap(u, TO_OTHER_CHIP)
    w_other = swap(w, TO_OTHER_CORE)
    h_near = swap(h_near, TO_OTHER_CORE)
    u_near = swap(u, TO_OTHER_CORE)
    h_far = swap(lax.dynamic_slice_in_dim(h_got, (1 - core) * rows, rows, 1), TO_OTHER_CORE)

    state = jnp.stack([global_params[0], outer_momentum[0]]).reshape(2, own_rows, NZ, lane)
    state = over(state.transpose(2, 0, 1, 3), Z_GROUPS)
    state = state.transpose(1, 0, 2, 3).reshape(2, half, lane)

    own = lax.dynamic_slice_in_dim(w, x_at * block, block, 0)
    sum_x = sum_over_x([own] + got, h_got)
    parts = over(sum_x.reshape(PLANE, half, lane), HZ_GROUPS)
    far_sent, near = project(at, h_got, h, w, w_other, factor, sum_x)
    u_got = hold(u_got, far_sent)
    u_far = swap(u_got, TO_OTHER_CORE)
    renewed, outer = outer_step(parts, state, lax.axis_size("rep"), u_got)
    upstreams = [u, u_near, u_got, u_far]
    kept = inner_step(
        at, h, h_near, h_got, h_far, upstreams, w, moment_one[0], moment_two[0], factor, renewed
    )
    spread = [over(renewed, HZ_GROUPS)]
    for d in range(1, NX):
        spread.append(swap(spread[0], TO_X[d]))

    values, outer = finish(near, swap(far_sent, TO_OTHER_CHIP), outer)
    outer = outer.reshape(2, NZ, own_rows, lane).transpose(1, 0, 2, 3)
    outer = over(outer, Z_GROUPS).transpose(1, 2, 0, 3).reshape(2, own_rows, cols)
    merged = merge(at, kept, spread)
    return (values[None], merged[None], outer[0][None], outer[1][None])


def solution(mesh):
    return jax.shard_map(
        on_device,
        mesh=mesh,
        in_specs=(
            P("rep", "fsdp", None),
            P("rep", "fsdp", None),
            P("rep", "fsdp", None),
            P("rep", "fsdp", None),
            P("rep", "fsdp", None),
            P("fsdp", "rep", None),
            P("fsdp", "rep", None),
        ),
        out_specs=(
            P("rep", "fsdp", None),
            P("rep", "fsdp", None),
            P("fsdp", "rep", None),
            P("fsdp", "rep", None),
        ),
        check_vma=False,
    )
```

```python
import jax
import jax.numpy as jnp
from jax import lax
from jax.experimental import pallas as pl
from jax.experimental.pallas import tpu as pltpu
from jax.sharding import PartitionSpec as P

beta_one = 0.9
beta_two = 0.95
bias_one = 1.0 - 0.9**8
bias_two = 1.0 - 0.95**8
inner_rate = 0.25
decay_rate = 0.1
epsilon = 1e-08
outer_rate = 0.7
outer_mu = 0.9
mixing = 0.5

NX, NYH, NZ = 4, 2, 8
NYL, NC = 2, 2
BOTH = ("rep", "fsdp")
PLANE = NYH * NZ
HZ_GROUPS = [[x * PLANE + k for k in range(PLANE)] for x in range(NX)]
BACK_GROUPS = [group[::-1] for group in HZ_GROUPS]


def pairs(move):
    found = []
    for x in range(NX):
        for h in range(NYH):
            for z in range(NZ):
                for y in range(NYL):
                    for c in range(NC):
                        x2, y2, c2 = move(x, y, c)
                        found.append(
                            (
                                ((x * NYH + h) * NZ + z) * 4 + y * 2 + c,
                                ((x2 * NYH + h) * NZ + z) * 4 + y2 * 2 + c2,
                            )
                        )
    return found


TO_OTHER_CORE = pairs(lambda x, y, c: (x, y, 1 - c))
TO_OTHER_CHIP = pairs(lambda x, y, c: (x, 1 - y, c))
TO_X = [pairs(lambda x, y, c, d=d: ((x + d) % NX, y, c)) for d in range(NX)]

MIB = 1024 * 1024
BF16, F32 = jnp.bfloat16, jnp.float32


def over(array, groups):
    return lax.all_to_all(array, "rep", 0, 0, axis_index_groups=groups)


def swap(array, to):
    return lax.ppermute(array, BOTH, to)


def dot(a, b):
    return jnp.dot(a, b, preferred_element_type=F32)


def dot_t(a, b):
    return lax.dot_general(a, b, (((0,), (0,)), ((), ())), preferred_element_type=F32)


def inside(array):
    return pltpu.with_memory_space_constraint(array, pltpu.VMEM)


def outside(array):
    return pltpu.with_memory_space_constraint(array, pltpu.HBM)


def call(kernel, grid, in_specs, out_specs, out_shape, flops, moved, at, *operands):
    spec = pltpu.PrefetchScalarGridSpec(
        num_scalar_prefetch=1, grid=grid, in_specs=in_specs, out_specs=out_specs
    )
    return pl.pallas_call(
        kernel,
        grid_spec=spec,
        out_shape=out_shape,
        compiler_params=pltpu.CompilerParams(vmem_limit_bytes=48 * MIB),
        cost_estimate=pl.CostEstimate(flops=flops, bytes_accessed=moved, transcendentals=0),
    )(at, *operands)


def cut(at, w, h):
    rows, cols = w.shape
    toks = h.shape[0]
    block, chip = rows // NX, rows * NC
    shapes = [(block, cols)] * (NX - 1) + [(toks, chip), (toks, rows)]
    count = len(shapes)

    def kernel(at_ref, w_ref, h_ref, *rest):
        outs, held, (in_sems, out_sems) = rest[:count], rest[count : 2 * count], rest[2 * count :]
        sources = []
        for d in range(1, NX):
            base = pl.multiple_of(lax.rem(at_ref[0] + d, NX) * block, 16)
            sources.append(w_ref.at[pl.ds(base, block)])
        far, near = (1 - at_ref[5]) * chip, at_ref[3] * rows
        sources.append(h_ref.at[:, pl.ds(pl.multiple_of(far, 128), chip)])
        sources.append(h_ref.at[:, pl.ds(pl.multiple_of(near, 128), rows)])
        ins = [pltpu.make_async_copy(sources[k], held[k], in_sems.at[k]) for k in range(count)]
        backs = [pltpu.make_async_copy(held[k], outs[k], out_sems.at[k]) for k in range(count)]
        for copy in ins:
            copy.start()
        for copy, back in zip(ins, backs, strict=True):
            copy.wait()
            back.start()
        for back in backs:
            back.wait()

    hbm = pl.BlockSpec(memory_space=pl.ANY)
    return pl.pallas_call(
        kernel,
        in_specs=[pl.BlockSpec(memory_space=pltpu.SMEM), hbm, hbm],
        out_specs=[hbm] * count,
        out_shape=[pltpu.HBM(x, BF16) for x in shapes],
        scratch_shapes=[pltpu.VMEM(x, BF16) for x in shapes]
        + [pltpu.SemaphoreType.DMA((count,)), pltpu.SemaphoreType.DMA((count,))],
        compiler_params=pltpu.CompilerParams(vmem_limit_bytes=12 * MIB),
    )(at, outside(w), outside(h))


def to_piece(rows_in, lane):
    return jnp.concatenate(
        [rows_in[:, c : c + lane] for c in range(0, rows_in.shape[1], lane)], axis=0
    )


def from_piece(piece, own):
    return jnp.concatenate(
        [piece[k : k + own] for k in range(0, piece.shape[0], own)], axis=1
    )


def sum_over_x(blocks, own, after):
    block, cols = blocks[0].shape
    half, lane = block // NYH, 128
    tall = own * cols // lane

    def kernel(w_ref, a_ref, b_ref, c_ref, after_ref, o_ref, held, sems):
        copies = []
        for i in range(NYH):
            rows = pl.ds(i * half, half)
            total = w_ref[rows].astype(F32) + a_ref[rows].astype(F32)
            total = total + (b_ref[rows].astype(F32) + c_ref[rows].astype(F32))
            for z in range(NZ):
                held[PLANE - 1 - i * NZ - z] = to_piece(total[z * own : (z + 1) * own], lane).astype(BF16)
            here = pl.ds((NYH - 1 - i) * NZ, NZ)
            copies.append(pltpu.make_async_copy(held.at[here], o_ref.at[here], sems.at[i]))
            copies[-1].start()
        for copy in copies:
            copy.wait()

    shape = (PLANE, tall, lane)
    return pl.pallas_call(
        kernel,
        in_specs=[pl.BlockSpec(memory_space=pltpu.VMEM)] * NX + [pl.BlockSpec(memory_space=pl.ANY)],
        out_specs=pl.BlockSpec(memory_space=pl.ANY),
        out_shape=pltpu.HBM(shape, BF16),
        scratch_shapes=[pltpu.VMEM(shape, BF16), pltpu.SemaphoreType.DMA((NYH,))],
        compiler_params=pltpu.CompilerParams(vmem_limit_bytes=16 * MIB),
    )(*[inside(x) for x in blocks], after)


def outer_step(parts, params, momenta, replicas, after):
    plane, tall, lane = parts.shape
    own = params.shape[0]

    def kernel(p_ref, g_hbm, m_hbm, after_ref, r_ref, new_ref, mom_ref, g_ref, m_ref, held, in_sems, sems):
        state = [
            pltpu.make_async_copy(g_hbm, g_ref, in_sems.at[0]),
            pltpu.make_async_copy(m_hbm, m_ref, in_sems.at[1]),
        ]
        for copy in state:
            copy.start()
        summed = p_ref[0].astype(F32)
        for k in range(1, plane):
            summed = summed + p_ref[k].astype(F32)
        summed = from_piece(summed, own)
        for copy in state:
            copy.wait()
        pseudo = g_ref[...] - summed / replicas
        momentum = outer_mu * m_ref[...] + pseudo
        renewed = g_ref[...] - outer_rate * (pseudo + outer_mu * momentum)
        held[...] = to_piece(renewed, lane).astype(BF16)
        copies = [pltpu.make_async_copy(held, r_ref.at[k], sems.at[k]) for k in range(plane)]
        for copy in copies:
            copy.start()
        new_ref[...] = renewed
        mom_ref[...] = momentum
        for copy in copies:
            copy.wait()

    vmem = pl.BlockSpec(memory_space=pltpu.VMEM)
    hbm = pl.BlockSpec(memory_space=pl.ANY)
    return pl.pallas_call(
        kernel,
        in_specs=[vmem, hbm, hbm, vmem],
        out_specs=[hbm, vmem, vmem],
        out_shape=[pltpu.HBM(parts.shape, BF16)] + [pltpu.HBM(params.shape, F32)] * 2,
        scratch_shapes=[
            pltpu.VMEM(params.shape, F32),
            pltpu.VMEM(params.shape, F32),
            pltpu.VMEM((tall, lane), BF16),
            pltpu.SemaphoreType.DMA((2,)),
            pltpu.SemaphoreType.DMA((plane,)),
        ],
        compiler_params=pltpu.CompilerParams(vmem_limit_bytes=8 * MIB),
    )(inside(parts), outside(params), outside(momenta), after)


def pack(pieces, own, after):
    plane, tall, lane = pieces.shape
    half, cols = NZ * own, tall // own * lane

    def kernel(p_ref, after_ref, o_ref, held, sems):
        copies = []
        for i in range(NYH):
            parts = [from_piece(p_ref[i * NZ + z].astype(F32), own) for z in range(NZ)]
            rows = pl.ds(i * half, half)
            held[rows] = jnp.concatenate(parts, axis=0).astype(BF16)
            copies.append(pltpu.make_async_copy(held.at[rows], o_ref.at[rows], sems.at[i]))
            copies[-1].start()
        for copy in copies:
            copy.wait()

    return pl.pallas_call(
        kernel,
        in_specs=[pl.BlockSpec(memory_space=pltpu.VMEM), pl.BlockSpec(memory_space=pl.ANY)],
        out_specs=pl.BlockSpec(memory_space=pl.ANY),
        out_shape=pltpu.HBM((NYH * half, cols), BF16),
        scratch_shapes=[pltpu.VMEM((NYH * half, cols), BF16), pltpu.SemaphoreType.DMA((NYH,))],
        compiler_params=pltpu.CompilerParams(vmem_limit_bytes=8 * MIB),
    )(inside(pieces), after)


def project(at, got, hidden, w, w_other, factor, after):
    rows, cols = w.shape
    toks = got.shape[0]
    steps = 4
    wide = cols // steps

    def kernel(at_ref, a_ref, b_ref, c_ref, d_ref, w_ref, v_ref, after_ref, far_ref, near_ref):
        far_ref[...] = ((dot(a_ref[...], w_ref[...]) + dot(b_ref[...], v_ref[...])) * factor).astype(BF16)
        near_ref[...] = (dot(c_ref[...], w_ref[...]) + dot(d_ref[...], v_ref[...])) * factor

    def left(k):
        return pl.BlockSpec((toks, rows), lambda i, at: (0, at[k]))

    column = pl.BlockSpec((toks, wide), lambda i, at: (0, i))
    wspec = pl.BlockSpec((rows, wide), lambda i, at: (0, i))
    return call(
        kernel,
        (steps,),
        [left(2), left(4), left(1), left(3), wspec, wspec, pl.BlockSpec(memory_space=pl.ANY)],
        [column, column],
        [jax.ShapeDtypeStruct((toks, cols), BF16), jax.ShapeDtypeStruct((toks, cols), F32)],
        8 * toks * rows * cols,
        4 * rows * cols + 8 * toks * rows,
        at,
        got,
        got,
        outside(hidden),
        outside(hidden),
        outside(w),
        outside(w_other),
        after,
    )


def hold(array, *after):
    hbm = pl.BlockSpec(memory_space=pl.ANY)
    small = (8, 128)

    def kernel(*refs):
        refs[-1][...] = jnp.zeros(small, F32)

    return pl.pallas_call(
        kernel,
        in_specs=[hbm] * (1 + len(after)),
        out_specs=[hbm, pl.BlockSpec(memory_space=pltpu.VMEM)],
        out_shape=[
            jax.ShapeDtypeStruct(array.shape, array.dtype),
            jax.ShapeDtypeStruct(small, F32),
        ],
        input_output_aliases={0: 0},
        compiler_params=pltpu.CompilerParams(vmem_limit_bytes=MIB),
    )(array, *after)


def finish(near, far):
    def kernel(n_ref, f_ref, o_ref):
        o_ref[...] = (n_ref[...] + f_ref[...].astype(F32)).astype(BF16)

    vmem = pl.BlockSpec(memory_space=pltpu.VMEM)
    return pl.pallas_call(
        kernel,
        in_specs=[vmem, vmem],
        out_specs=vmem,
        out_shape=jax.ShapeDtypeStruct(near.shape, BF16),
        compiler_params=pltpu.CompilerParams(vmem_limit_bytes=16 * MIB),
    )(near, far)


def inner_step(at, hidden, near, far_got, far, upstreams, w, m1, m2, factor):
    rows, cols = w.shape
    toks = hidden.shape[0]
    tall = 384
    steps = rows // tall

    def kernel(at_ref, h_ref, n_ref, g_ref, f_ref, hu_ref, nu_ref, gu_ref, fu_ref, w_ref, m1_ref, m2_ref, o_ref):
        gradient = dot_t(h_ref[...], hu_ref[...]) + dot_t(n_ref[...], nu_ref[...])
        gradient = gradient + dot_t(g_ref[...], gu_ref[...]) + dot_t(f_ref[...], fu_ref[...])
        gradient = gradient * factor
        moment_new = beta_one * m1_ref[...].astype(F32) + (1.0 - beta_one) * gradient
        second_new = beta_two * m2_ref[...].astype(F32) + (1.0 - beta_two) * gradient * gradient
        scale = jnp.sqrt(second_new * (1.0 / bias_two)) + epsilon
        stepped = moment_new * (mixing * inner_rate / bias_one) / scale
        o_ref[...] = (mixing * (1.0 - inner_rate * decay_rate)) * w_ref[...].astype(F32) - stepped

    def left(first):
        return pl.BlockSpec((toks, tall), first)

    whole = pl.BlockSpec((toks, cols), lambda i, at: (0, 0))
    own = pl.BlockSpec((tall, cols), lambda i, at: (i, 0))
    spec = pltpu.PrefetchScalarGridSpec(
        num_scalar_prefetch=1,
        grid=(steps,),
        in_specs=[
            left(lambda i, at: (0, at[1] * steps + i)),
            left(lambda i, at: (0, i)),
            left(lambda i, at: (0, at[2] * steps + i)),
            left(lambda i, at: (0, i)),
            whole,
            whole,
            whole,
            whole,
            own,
            own,
            own,
        ],
        out_specs=own,
    )
    operands = [outside(hidden), near, far_got, far] + upstreams + [outside(w), outside(m1), outside(m2)]
    return pl.pallas_call(
        kernel,
        grid_spec=spec,
        out_shape=pltpu.HBM((rows, cols), F32),
        compiler_params=pltpu.CompilerParams(vmem_limit_bytes=40 * MIB),
        cost_estimate=pl.CostEstimate(
            flops=8 * toks * rows * cols, bytes_accessed=10 * rows * cols, transcendentals=0
        ),
    )(at, *operands)


def merge(at, kept, spread):
    rows, cols = kept.shape
    block = rows // NX

    def kernel(at_ref, k_ref, a_ref, b_ref, c_ref, d_ref, o_ref, kept_ref, held, in_sems, out_sems):
        refs = [a_ref, b_ref, c_ref, d_ref]
        places = [pl.ds(pl.multiple_of(lax.rem(at_ref[0] + NX - d, NX) * block, 16), block) for d in range(NX)]
        ins = [pltpu.make_async_copy(k_ref.at[places[d]], kept_ref.at[d], in_sems.at[d]) for d in range(NX)]
        outs = [pltpu.make_async_copy(held.at[d], o_ref.at[places[d]], out_sems.at[d]) for d in range(NX)]
        for copy in ins:
            copy.start()
        for d in range(NX):
            ins[d].wait()
            new = (1.0 - mixing) * refs[d][...].astype(F32)
            held[d] = (kept_ref[d] + new).astype(BF16)
            outs[d].start()
        for copy in outs:
            copy.wait()

    vmem, hbm = pl.BlockSpec(memory_space=pltpu.VMEM), pl.BlockSpec(memory_space=pl.ANY)
    return pl.pallas_call(
        kernel,
        in_specs=[pl.BlockSpec(memory_space=pltpu.SMEM), hbm] + [vmem] * NX,
        out_specs=hbm,
        out_shape=jax.ShapeDtypeStruct((rows, cols), BF16),
        scratch_shapes=[
            pltpu.VMEM((NX, block, cols), F32),
            pltpu.VMEM((NX, block, cols), BF16),
            pltpu.SemaphoreType.DMA((NX,)),
            pltpu.SemaphoreType.DMA((NX,)),
        ],
        compiler_params=pltpu.CompilerParams(vmem_limit_bytes=24 * MIB),
        cost_estimate=pl.CostEstimate(flops=2 * rows * cols, bytes_accessed=8 * rows * cols, transcendentals=0),
    )(at, outside(kept), *[inside(x) for x in spread])


def on_device(hidden, upstream, weights, moment_one, moment_two, global_params, outer_momentum):
    width = hidden.shape[2]
    rows = weights.shape[1]
    factor = float(width) ** (-0.5)
    own = global_params.shape[1]
    block = rows // NX
    rep, fsdp = lax.axis_index("rep"), lax.axis_index("fsdp")
    core, pair = fsdp % NC, fsdp // NC
    x_at = rep // PLANE
    sibling = pair * NC + 1 - core
    at = jnp.stack([x_at, fsdp, core, sibling, 1 - core, pair]).astype(jnp.int32)
    w, h, u = weights[0], hidden[0], upstream[0]

    *sent, h_sent, h_near = cut(at, w, h)
    got = [swap(x, TO_X[d]) for d, x in enumerate(sent, 1)]

    w_other = swap(w, TO_OTHER_CORE)
    h_got = swap(h_sent, TO_OTHER_CHIP)
    h_near = swap(h_near, TO_OTHER_CORE)
    u_near = swap(u, TO_OTHER_CORE)
    h_far = swap(lax.dynamic_slice_in_dim(h_got, (1 - core) * rows, rows, 1), TO_OTHER_CORE)

    mine = lax.dynamic_slice_in_dim(w, x_at * block, block, 0)
    sum_x = sum_over_x([mine] + got, own, h_got)
    parts = over(sum_x, BACK_GROUPS)
    far_sent, near = project(at, h_got, h, w, w_other, factor, sum_x)
    u_got, token = hold(swap(u, TO_OTHER_CHIP), far_sent)
    u_far = swap(u_got, TO_OTHER_CORE)
    renewed, new_global, new_momentum = outer_step(
        parts, global_params[0], outer_momentum[0], lax.axis_size("rep"), token
    )
    corners = jnp.stack([x[:8, :128] for x in (u_far, h_far)])
    spread = [pack(over(renewed, HZ_GROUPS), own, corners)]
    for d in range(1, NX):
        spread.append(swap(spread[0], TO_X[d]))

    upstreams = [u, u_near, u_got, u_far]
    kept = inner_step(at, h, h_near, h_got, h_far, upstreams, w, moment_one[0], moment_two[0], factor)
    values = finish(near, swap(far_sent, TO_OTHER_CHIP))
    merged = merge(at, kept, spread)
    return (values[None], merged[None], new_global[None], new_momentum[None])


def solution(mesh):
    return jax.shard_map(
        on_device,
        mesh=mesh,
        in_specs=(
            P("rep", "fsdp", None),
            P("rep", "fsdp", None),
            P("rep", "fsdp", None),
            P("rep", "fsdp", None),
            P("rep", "fsdp", None),
            P("fsdp", "rep", None),
            P("fsdp", "rep", None),
        ),
        out_specs=(
            P("rep", "fsdp", None),
            P("rep", "fsdp", None),
            P("fsdp", "rep", None),
            P("fsdp", "rep", None),
        ),
        check_vma=False,
    )
```

```python
import jax
import jax.numpy as jnp
from jax import lax
from jax.experimental import pallas as pl
from jax.experimental.pallas import tpu as pltpu
from jax.sharding import PartitionSpec as P

beta_one = 0.9
beta_two = 0.95
bias_one = 1.0 - 0.9**8
bias_two = 1.0 - 0.95**8
inner_rate = 0.25
decay_rate = 0.1
epsilon = 1e-08
outer_rate = 0.7
outer_mu = 0.9
mixing = 0.5

NX, NYH, NZ = 4, 2, 8
NYL, NC = 2, 2
BOTH = ("rep", "fsdp")
PLANE = NYH * NZ
HZ_GROUPS = [[x * PLANE + k for k in range(PLANE)] for x in range(NX)]
BACK_GROUPS = [group[::-1] for group in HZ_GROUPS]


def pairs(move):
    found = []
    for x in range(NX):
        for h in range(NYH):
            for z in range(NZ):
                for y in range(NYL):
                    for c in range(NC):
                        x2, y2, c2 = move(x, y, c)
                        found.append(
                            (
                                ((x * NYH + h) * NZ + z) * 4 + y * 2 + c,
                                ((x2 * NYH + h) * NZ + z) * 4 + y2 * 2 + c2,
                            )
                        )
    return found


TO_OTHER_CORE = pairs(lambda x, y, c: (x, y, 1 - c))
TO_OTHER_CHIP = pairs(lambda x, y, c: (x, 1 - y, c))
TO_X = [pairs(lambda x, y, c, d=d: ((x + d) % NX, y, c)) for d in range(NX)]

MIB = 1024 * 1024
BF16, F32 = jnp.bfloat16, jnp.float32


def over(array, groups):
    return lax.all_to_all(array, "rep", 0, 0, axis_index_groups=groups)


def swap(array, to):
    return lax.ppermute(array, BOTH, to)


def dot(a, b):
    return jnp.dot(a, b, preferred_element_type=F32)


def dot_t(a, b):
    return lax.dot_general(a, b, (((0,), (0,)), ((), ())), preferred_element_type=F32)


def inside(array):
    return pltpu.with_memory_space_constraint(array, pltpu.VMEM)


def outside(array):
    return pltpu.with_memory_space_constraint(array, pltpu.HBM)


def call(kernel, grid, in_specs, out_specs, out_shape, flops, moved, at, *operands):
    spec = pltpu.PrefetchScalarGridSpec(
        num_scalar_prefetch=1, grid=grid, in_specs=in_specs, out_specs=out_specs
    )
    return pl.pallas_call(
        kernel,
        grid_spec=spec,
        out_shape=out_shape,
        compiler_params=pltpu.CompilerParams(vmem_limit_bytes=48 * MIB),
        cost_estimate=pl.CostEstimate(flops=flops, bytes_accessed=moved, transcendentals=0),
    )(at, *operands)


def cut(at, w, h):
    rows, cols = w.shape
    toks = h.shape[0]
    block, chip = rows // NX, rows * NC
    shapes = [(block, cols)] * (NX - 1) + [(toks, chip), (toks, rows)]
    count = len(shapes)

    def kernel(at_ref, w_ref, h_ref, *rest):
        outs, held, (in_sems, out_sems) = rest[:count], rest[count : 2 * count], rest[2 * count :]
        sources = []
        for d in range(1, NX):
            base = pl.multiple_of(lax.rem(at_ref[0] + d, NX) * block, 16)
            sources.append(w_ref.at[pl.ds(base, block)])
        far, near = (1 - at_ref[5]) * chip, at_ref[3] * rows
        sources.append(h_ref.at[:, pl.ds(pl.multiple_of(far, 128), chip)])
        sources.append(h_ref.at[:, pl.ds(pl.multiple_of(near, 128), rows)])
        ins = [pltpu.make_async_copy(sources[k], held[k], in_sems.at[k]) for k in range(count)]
        backs = [pltpu.make_async_copy(held[k], outs[k], out_sems.at[k]) for k in range(count)]
        for copy in ins:
            copy.start()
        for copy, back in zip(ins, backs, strict=True):
            copy.wait()
            back.start()
        for back in backs:
            back.wait()

    hbm = pl.BlockSpec(memory_space=pl.ANY)
    return pl.pallas_call(
        kernel,
        in_specs=[pl.BlockSpec(memory_space=pltpu.SMEM), hbm, hbm],
        out_specs=[hbm] * count,
        out_shape=[pltpu.HBM(x, BF16) for x in shapes],
        scratch_shapes=[pltpu.VMEM(x, BF16) for x in shapes]
        + [pltpu.SemaphoreType.DMA((count,)), pltpu.SemaphoreType.DMA((count,))],
        compiler_params=pltpu.CompilerParams(vmem_limit_bytes=12 * MIB),
    )(at, outside(w), outside(h))


def to_piece(rows_in, lane):
    return jnp.concatenate(
        [rows_in[:, c : c + lane] for c in range(0, rows_in.shape[1], lane)], axis=0
    )


def from_piece(piece, own):
    return jnp.concatenate(
        [piece[k : k + own] for k in range(0, piece.shape[0], own)], axis=1
    )


def sum_over_x(blocks, own, after):
    block, cols = blocks[0].shape
    half, lane = block // NYH, 128
    tall = own * cols // lane

    def kernel(w_ref, a_ref, b_ref, c_ref, after_ref, o_ref, held, sems):
        copies = []
        for i in range(NYH):
            rows = pl.ds(i * half, half)
            total = w_ref[rows].astype(F32) + a_ref[rows].astype(F32)
            total = total + (b_ref[rows].astype(F32) + c_ref[rows].astype(F32))
            for z in range(NZ):
                held[PLANE - 1 - i * NZ - z] = to_piece(total[z * own : (z + 1) * own], lane).astype(BF16)
            here = pl.ds((NYH - 1 - i) * NZ, NZ)
            copies.append(pltpu.make_async_copy(held.at[here], o_ref.at[here], sems.at[i]))
            copies[-1].start()
        for copy in copies:
            copy.wait()

    shape = (PLANE, tall, lane)
    return pl.pallas_call(
        kernel,
        in_specs=[pl.BlockSpec(memory_space=pltpu.VMEM)] * NX + [pl.BlockSpec(memory_space=pl.ANY)],
        out_specs=pl.BlockSpec(memory_space=pl.ANY),
        out_shape=pltpu.HBM(shape, BF16),
        scratch_shapes=[pltpu.VMEM(shape, BF16), pltpu.SemaphoreType.DMA((NYH,))],
        compiler_params=pltpu.CompilerParams(vmem_limit_bytes=16 * MIB),
    )(*[inside(x) for x in blocks], after)


def outer_step(parts, params, momenta, replicas, after):
    plane, tall, lane = parts.shape
    own = params.shape[0]

    def kernel(p_ref, g_hbm, m_hbm, after_ref, r_ref, new_ref, mom_ref, g_ref, m_ref, held, in_sems, sems):
        state = [
            pltpu.make_async_copy(g_hbm, g_ref, in_sems.at[0]),
            pltpu.make_async_copy(m_hbm, m_ref, in_sems.at[1]),
        ]
        for copy in state:
            copy.start()
        summed = p_ref[0].astype(F32)
        for k in range(1, plane):
            summed = summed + p_ref[k].astype(F32)
        summed = from_piece(summed, own)
        for copy in state:
            copy.wait()
        pseudo = g_ref[...] - summed / replicas
        momentum = outer_mu * m_ref[...] + pseudo
        renewed = g_ref[...] - outer_rate * (pseudo + outer_mu * momentum)
        held[...] = to_piece(renewed, lane).astype(BF16)
        copies = [pltpu.make_async_copy(held, r_ref.at[k], sems.at[k]) for k in range(plane)]
        for copy in copies:
            copy.start()
        new_ref[...] = renewed
        mom_ref[...] = momentum
        for copy in copies:
            copy.wait()

    vmem = pl.BlockSpec(memory_space=pltpu.VMEM)
    hbm = pl.BlockSpec(memory_space=pl.ANY)
    return pl.pallas_call(
        kernel,
        in_specs=[vmem, hbm, hbm, vmem],
        out_specs=[hbm, vmem, vmem],
        out_shape=[pltpu.HBM(parts.shape, BF16)] + [pltpu.HBM(params.shape, F32)] * 2,
        scratch_shapes=[
            pltpu.VMEM(params.shape, F32),
            pltpu.VMEM(params.shape, F32),
            pltpu.VMEM((tall, lane), BF16),
            pltpu.SemaphoreType.DMA((2,)),
            pltpu.SemaphoreType.DMA((plane,)),
        ],
        compiler_params=pltpu.CompilerParams(vmem_limit_bytes=8 * MIB),
    )(inside(parts), outside(params), outside(momenta), after)


def pack(pieces, own, after):
    plane, tall, lane = pieces.shape
    half, cols = NZ * own, tall // own * lane

    def kernel(p_ref, after_ref, o_ref, held, sems):
        copies = []
        for i in range(NYH):
            parts = [from_piece(p_ref[i * NZ + z].astype(F32), own) for z in range(NZ)]
            rows = pl.ds(i * half, half)
            held[rows] = jnp.concatenate(parts, axis=0).astype(BF16)
            copies.append(pltpu.make_async_copy(held.at[rows], o_ref.at[rows], sems.at[i]))
            copies[-1].start()
        for copy in copies:
            copy.wait()

    return pl.pallas_call(
        kernel,
        in_specs=[pl.BlockSpec(memory_space=pltpu.VMEM), pl.BlockSpec(memory_space=pl.ANY)],
        out_specs=pl.BlockSpec(memory_space=pl.ANY),
        out_shape=pltpu.HBM((NYH * half, cols), BF16),
        scratch_shapes=[pltpu.VMEM((NYH * half, cols), BF16), pltpu.SemaphoreType.DMA((NYH,))],
        compiler_params=pltpu.CompilerParams(vmem_limit_bytes=8 * MIB),
    )(inside(pieces), after)


def project(at, got, hidden, w, w_other, factor, after):
    rows, cols = w.shape
    toks = got.shape[0]
    steps = 4
    wide = cols // steps

    def kernel(at_ref, a_ref, b_ref, c_ref, d_ref, w_ref, v_ref, after_ref, far_ref, near_ref):
        far_ref[...] = ((dot(a_ref[...], w_ref[...]) + dot(b_ref[...], v_ref[...])) * factor).astype(BF16)
        near_ref[...] = (dot(c_ref[...], w_ref[...]) + dot(d_ref[...], v_ref[...])) * factor

    def left(k):
        return pl.BlockSpec((toks, rows), lambda i, at: (0, at[k]))

    column = pl.BlockSpec((toks, wide), lambda i, at: (0, i))
    wspec = pl.BlockSpec((rows, wide), lambda i, at: (0, i))
    return call(
        kernel,
        (steps,),
        [left(2), left(4), left(1), left(3), wspec, wspec, pl.BlockSpec(memory_space=pl.ANY)],
        [column, column],
        [pltpu.HBM((toks, cols), BF16), jax.ShapeDtypeStruct((toks, cols), F32)],
        8 * toks * rows * cols,
        4 * rows * cols + 8 * toks * rows,
        at,
        got,
        got,
        outside(hidden),
        outside(hidden),
        outside(w),
        outside(w_other),
        after,
    )


def hold(array, *after):
    hbm = pl.BlockSpec(memory_space=pl.ANY)
    small = (8, 128)

    def kernel(*refs):
        refs[-1][...] = jnp.zeros(small, F32)

    return pl.pallas_call(
        kernel,
        in_specs=[hbm] * (1 + len(after)),
        out_specs=[hbm, pl.BlockSpec(memory_space=pltpu.VMEM)],
        out_shape=[
            jax.ShapeDtypeStruct(array.shape, array.dtype),
            jax.ShapeDtypeStruct(small, F32),
        ],
        input_output_aliases={0: 0},
        compiler_params=pltpu.CompilerParams(vmem_limit_bytes=MIB),
    )(array, *after)


def finish(near, far):
    def kernel(n_ref, f_ref, o_ref):
        o_ref[...] = (n_ref[...] + f_ref[...].astype(F32)).astype(BF16)

    vmem = pl.BlockSpec(memory_space=pltpu.VMEM)
    return pl.pallas_call(
        kernel,
        in_specs=[vmem, vmem],
        out_specs=vmem,
        out_shape=jax.ShapeDtypeStruct(near.shape, BF16),
        compiler_params=pltpu.CompilerParams(vmem_limit_bytes=16 * MIB),
    )(near, far)


def inner_step(at, hidden, near, far_got, far, upstreams, w, m1, m2, factor):
    rows, cols = w.shape
    toks = hidden.shape[0]
    tall = 384
    steps = rows // tall

    def kernel(at_ref, h_ref, n_ref, g_ref, f_ref, hu_ref, nu_ref, gu_ref, fu_ref, w_ref, m1_ref, m2_ref, o_ref):
        gradient = dot_t(h_ref[...], hu_ref[...]) + dot_t(n_ref[...], nu_ref[...])
        gradient = gradient + dot_t(g_ref[...], gu_ref[...]) + dot_t(f_ref[...], fu_ref[...])
        gradient = gradient * factor
        moment_new = beta_one * m1_ref[...].astype(F32) + (1.0 - beta_one) * gradient
        second_new = beta_two * m2_ref[...].astype(F32) + (1.0 - beta_two) * gradient * gradient
        scale = jnp.sqrt(second_new * (1.0 / bias_two)) + epsilon
        stepped = moment_new * (mixing * inner_rate / bias_one) / scale
        half = (mixing * (1.0 - inner_rate * decay_rate)) * w_ref[...].astype(F32) - stepped
        o_ref[...] = half.astype(BF16)

    def left(first):
        return pl.BlockSpec((toks, tall), first)

    whole = pl.BlockSpec((toks, cols), lambda i, at: (0, 0))
    own = pl.BlockSpec((tall, cols), lambda i, at: (i, 0))
    spec = pltpu.PrefetchScalarGridSpec(
        num_scalar_prefetch=1,
        grid=(steps,),
        in_specs=[
            left(lambda i, at: (0, at[1] * steps + i)),
            left(lambda i, at: (0, i)),
            left(lambda i, at: (0, at[2] * steps + i)),
            left(lambda i, at: (0, i)),
            whole,
            whole,
            whole,
            whole,
            own,
            own,
            own,
        ],
        out_specs=own,
    )
    operands = [outside(hidden), near, far_got, far] + upstreams + [outside(w), outside(m1), outside(m2)]
    return pl.pallas_call(
        kernel,
        grid_spec=spec,
        out_shape=pltpu.HBM((rows, cols), BF16),
        compiler_params=pltpu.CompilerParams(vmem_limit_bytes=40 * MIB),
        cost_estimate=pl.CostEstimate(
            flops=8 * toks * rows * cols, bytes_accessed=10 * rows * cols, transcendentals=0
        ),
    )(at, *operands)


def merge(at, kept, spread):
    rows, cols = kept.shape
    block = rows // NX

    def kernel(at_ref, k_ref, a_ref, b_ref, c_ref, d_ref, o_ref, kept_ref, held, in_sems, out_sems):
        refs = [a_ref, b_ref, c_ref, d_ref]
        places = [pl.ds(pl.multiple_of(lax.rem(at_ref[0] + NX - d, NX) * block, 16), block) for d in range(NX)]
        ins = [pltpu.make_async_copy(k_ref.at[places[d]], kept_ref.at[d], in_sems.at[d]) for d in range(NX)]
        outs = [pltpu.make_async_copy(held.at[d], o_ref.at[places[d]], out_sems.at[d]) for d in range(NX)]
        for copy in ins:
            copy.start()
        for d in range(NX):
            ins[d].wait()
            new = (1.0 - mixing) * refs[d][...].astype(F32)
            held[d] = (kept_ref[d].astype(F32) + new).astype(BF16)
            outs[d].start()
        for copy in outs:
            copy.wait()

    vmem, hbm = pl.BlockSpec(memory_space=pltpu.VMEM), pl.BlockSpec(memory_space=pl.ANY)
    return pl.pallas_call(
        kernel,
        in_specs=[pl.BlockSpec(memory_space=pltpu.SMEM), hbm] + [vmem] * NX,
        out_specs=hbm,
        out_shape=jax.ShapeDtypeStruct((rows, cols), BF16),
        scratch_shapes=[
            pltpu.VMEM((NX, block, cols), BF16),
            pltpu.VMEM((NX, block, cols), BF16),
            pltpu.SemaphoreType.DMA((NX,)),
            pltpu.SemaphoreType.DMA((NX,)),
        ],
        compiler_params=pltpu.CompilerParams(vmem_limit_bytes=24 * MIB),
        cost_estimate=pl.CostEstimate(flops=2 * rows * cols, bytes_accessed=8 * rows * cols, transcendentals=0),
    )(at, outside(kept), *[inside(x) for x in spread])


def on_device(hidden, upstream, weights, moment_one, moment_two, global_params, outer_momentum):
    width = hidden.shape[2]
    rows = weights.shape[1]
    factor = float(width) ** (-0.5)
    own = global_params.shape[1]
    block = rows // NX
    rep, fsdp = lax.axis_index("rep"), lax.axis_index("fsdp")
    core, pair = fsdp % NC, fsdp // NC
    x_at = rep // PLANE
    sibling = pair * NC + 1 - core
    at = jnp.stack([x_at, fsdp, core, sibling, 1 - core, pair]).astype(jnp.int32)
    w, h, u = weights[0], hidden[0], upstream[0]

    *sent, h_sent, h_near = cut(at, w, h)
    got = [swap(x, TO_X[d]) for d, x in enumerate(sent, 1)]

    w_other = swap(w, TO_OTHER_CORE)
    h_got = swap(h_sent, TO_OTHER_CHIP)
    h_near = swap(h_near, TO_OTHER_CORE)
    u_near = swap(u, TO_OTHER_CORE)
    h_far = swap(lax.dynamic_slice_in_dim(h_got, (1 - core) * rows, rows, 1), TO_OTHER_CORE)

    mine = lax.dynamic_slice_in_dim(w, x_at * block, block, 0)
    sum_x = sum_over_x([mine] + got, own, h_got)
    parts = over(sum_x, BACK_GROUPS)
    far_sent, near = project(at, h_got, h, w, w_other, factor, sum_x)
    u_got, token = hold(swap(u, TO_OTHER_CHIP), far_sent)
    u_far = swap(u_got, TO_OTHER_CORE)
    renewed, new_global, new_momentum = outer_step(
        parts, global_params[0], outer_momentum[0], lax.axis_size("rep"), token
    )
    corners = jnp.stack([x[:8, :128] for x in (u_far, h_far)])
    spread = [pack(over(renewed, HZ_GROUPS), own, corners)]
    for d in range(1, NX):
        spread.append(swap(spread[0], TO_X[d]))

    upstreams = [u, u_near, u_got, u_far]
    kept = inner_step(at, h, h_near, h_got, h_far, upstreams, w, moment_one[0], moment_two[0], factor)
    values = finish(near, swap(far_sent, TO_OTHER_CHIP))
    merged = merge(at, kept, spread)
    return (values[None], merged[None], new_global[None], new_momentum[None])


def solution(mesh):
    return jax.shard_map(
        on_device,
        mesh=mesh,
        in_specs=(
            P("rep", "fsdp", None),
            P("rep", "fsdp", None),
            P("rep", "fsdp", None),
            P("rep", "fsdp", None),
            P("rep", "fsdp", None),
            P("fsdp", "rep", None),
            P("fsdp", "rep", None),
        ),
        out_specs=(
            P("rep", "fsdp", None),
            P("rep", "fsdp", None),
            P("fsdp", "rep", None),
            P("fsdp", "rep", None),
        ),
        check_vma=False,
    )
```

```python
import jax
import jax.numpy as jnp
from jax import lax
from jax.experimental import pallas as pl
from jax.experimental.pallas import tpu as pltpu
from jax.sharding import PartitionSpec as P

beta_one = 0.9
beta_two = 0.95
bias_one = 1.0 - 0.9**8
bias_two = 1.0 - 0.95**8
inner_rate = 0.25
decay_rate = 0.1
epsilon = 1e-08
outer_rate = 0.7
outer_mu = 0.9
mixing = 0.5

NX, NYH, NZ = 4, 2, 8
NYL, NC = 2, 2
BOTH = ("rep", "fsdp")
PLANE = NYH * NZ
HZ_GROUPS = [[x * PLANE + k for k in range(PLANE)] for x in range(NX)]
BACK_GROUPS = [group[::-1] for group in HZ_GROUPS]


def pairs(move):
    found = []
    for x in range(NX):
        for h in range(NYH):
            for z in range(NZ):
                for y in range(NYL):
                    for c in range(NC):
                        x2, y2, c2 = move(x, y, c)
                        found.append(
                            (
                                ((x * NYH + h) * NZ + z) * 4 + y * 2 + c,
                                ((x2 * NYH + h) * NZ + z) * 4 + y2 * 2 + c2,
                            )
                        )
    return found


TO_OTHER_CORE = pairs(lambda x, y, c: (x, y, 1 - c))
TO_OTHER_CHIP = pairs(lambda x, y, c: (x, 1 - y, c))
TO_X = [pairs(lambda x, y, c, d=d: ((x + d) % NX, y, c)) for d in range(NX)]

MIB = 1024 * 1024
BF16, F32 = jnp.bfloat16, jnp.float32


def over(array, groups):
    return lax.all_to_all(array, "rep", 0, 0, axis_index_groups=groups)


def swap(array, to):
    return lax.ppermute(array, BOTH, to)


def dot(a, b):
    return jnp.dot(a, b, preferred_element_type=F32)


def dot_t(a, b):
    return lax.dot_general(a, b, (((0,), (0,)), ((), ())), preferred_element_type=F32)


def inside(array):
    return pltpu.with_memory_space_constraint(array, pltpu.VMEM)


def outside(array):
    return pltpu.with_memory_space_constraint(array, pltpu.HBM)


def call(kernel, grid, in_specs, out_specs, out_shape, flops, moved, at, *operands):
    spec = pltpu.PrefetchScalarGridSpec(
        num_scalar_prefetch=1, grid=grid, in_specs=in_specs, out_specs=out_specs
    )
    return pl.pallas_call(
        kernel,
        grid_spec=spec,
        out_shape=out_shape,
        compiler_params=pltpu.CompilerParams(vmem_limit_bytes=48 * MIB),
        cost_estimate=pl.CostEstimate(flops=flops, bytes_accessed=moved, transcendentals=0),
    )(at, *operands)


def cut(at, w, h):
    rows, cols = w.shape
    toks = h.shape[0]
    block, chip = rows // NX, rows * NC
    shapes = [(block, cols)] * (NX - 1) + [(toks, chip)]
    count = len(shapes)

    def kernel(at_ref, w_ref, h_ref, *rest):
        outs, held, (in_sems, out_sems) = rest[:count], rest[count : 2 * count], rest[2 * count :]
        sources = []
        for d in range(1, NX):
            base = pl.multiple_of(lax.rem(at_ref[0] + d, NX) * block, 16)
            sources.append(w_ref.at[pl.ds(base, block)])
        far = (1 - at_ref[5]) * chip
        sources.append(h_ref.at[:, pl.ds(pl.multiple_of(far, 128), chip)])
        ins = [pltpu.make_async_copy(sources[k], held[k], in_sems.at[k]) for k in range(count)]
        backs = [pltpu.make_async_copy(held[k], outs[k], out_sems.at[k]) for k in range(count)]
        for copy in ins:
            copy.start()
        for copy, back in zip(ins, backs, strict=True):
            copy.wait()
            back.start()
        for back in backs:
            back.wait()

    hbm = pl.BlockSpec(memory_space=pl.ANY)
    return pl.pallas_call(
        kernel,
        in_specs=[pl.BlockSpec(memory_space=pltpu.SMEM), hbm, hbm],
        out_specs=[hbm] * count,
        out_shape=[pltpu.HBM(x, BF16) for x in shapes],
        scratch_shapes=[pltpu.VMEM(x, BF16) for x in shapes]
        + [pltpu.SemaphoreType.DMA((count,)), pltpu.SemaphoreType.DMA((count,))],
        compiler_params=pltpu.CompilerParams(vmem_limit_bytes=12 * MIB),
    )(at, outside(w), outside(h))


def to_piece(rows_in, lane):
    return jnp.concatenate(
        [rows_in[:, c : c + lane] for c in range(0, rows_in.shape[1], lane)], axis=0
    )


def from_piece(piece, own):
    return jnp.concatenate(
        [piece[k : k + own] for k in range(0, piece.shape[0], own)], axis=1
    )


def sum_over_x(blocks, own, after):
    block, cols = blocks[0].shape
    half, lane = block // NYH, 128
    tall = own * cols // lane

    def kernel(w_ref, a_ref, b_ref, c_ref, after_ref, o_ref, held, sems):
        copies = []
        for i in range(NYH):
            rows = pl.ds(i * half, half)
            total = w_ref[rows].astype(F32) + a_ref[rows].astype(F32)
            total = total + (b_ref[rows].astype(F32) + c_ref[rows].astype(F32))
            for z in range(NZ):
                held[PLANE - 1 - i * NZ - z] = to_piece(total[z * own : (z + 1) * own], lane).astype(BF16)
            here = pl.ds((NYH - 1 - i) * NZ, NZ)
            copies.append(pltpu.make_async_copy(held.at[here], o_ref.at[here], sems.at[i]))
            copies[-1].start()
        for copy in copies:
            copy.wait()

    shape = (PLANE, tall, lane)
    return pl.pallas_call(
        kernel,
        in_specs=[pl.BlockSpec(memory_space=pltpu.VMEM)] * NX + [pl.BlockSpec(memory_space=pl.ANY)],
        out_specs=pl.BlockSpec(memory_space=pl.ANY),
        out_shape=pltpu.HBM(shape, BF16),
        scratch_shapes=[pltpu.VMEM(shape, BF16), pltpu.SemaphoreType.DMA((NYH,))],
        compiler_params=pltpu.CompilerParams(vmem_limit_bytes=16 * MIB),
    )(*[inside(x) for x in blocks], after)


def outer_step(parts, params, momenta, replicas, after):
    plane, tall, lane = parts.shape
    own = params.shape[0]

    def kernel(p_ref, g_hbm, m_hbm, after_ref, r_ref, new_ref, mom_ref, g_ref, m_ref, held, in_sems, sems):
        state = [
            pltpu.make_async_copy(g_hbm, g_ref, in_sems.at[0]),
            pltpu.make_async_copy(m_hbm, m_ref, in_sems.at[1]),
        ]
        for copy in state:
            copy.start()
        summed = p_ref[0].astype(F32)
        for k in range(1, plane):
            summed = summed + p_ref[k].astype(F32)
        summed = from_piece(summed, own)
        for copy in state:
            copy.wait()
        pseudo = g_ref[...] - summed / replicas
        momentum = outer_mu * m_ref[...] + pseudo
        renewed = g_ref[...] - outer_rate * (pseudo + outer_mu * momentum)
        held[...] = to_piece(renewed, lane).astype(BF16)
        copies = [pltpu.make_async_copy(held, r_ref.at[k], sems.at[k]) for k in range(plane)]
        for copy in copies:
            copy.start()
        new_ref[...] = renewed
        mom_ref[...] = momentum
        for copy in copies:
            copy.wait()

    vmem = pl.BlockSpec(memory_space=pltpu.VMEM)
    hbm = pl.BlockSpec(memory_space=pl.ANY)
    return pl.pallas_call(
        kernel,
        in_specs=[vmem, hbm, hbm, vmem],
        out_specs=[hbm, vmem, vmem],
        out_shape=[pltpu.HBM(parts.shape, BF16)] + [pltpu.HBM(params.shape, F32)] * 2,
        scratch_shapes=[
            pltpu.VMEM(params.shape, F32),
            pltpu.VMEM(params.shape, F32),
            pltpu.VMEM((tall, lane), BF16),
            pltpu.SemaphoreType.DMA((2,)),
            pltpu.SemaphoreType.DMA((plane,)),
        ],
        compiler_params=pltpu.CompilerParams(vmem_limit_bytes=8 * MIB),
    )(inside(parts), outside(params), outside(momenta), after)


def pack(pieces, own, after):
    plane, tall, lane = pieces.shape
    half, cols = NZ * own, tall // own * lane

    def kernel(p_ref, after_ref, o_ref, held, sems):
        copies = []
        for i in range(NYH):
            parts = [from_piece(p_ref[i * NZ + z].astype(F32), own) for z in range(NZ)]
            rows = pl.ds(i * half, half)
            held[rows] = jnp.concatenate(parts, axis=0).astype(BF16)
            copies.append(pltpu.make_async_copy(held.at[rows], o_ref.at[rows], sems.at[i]))
            copies[-1].start()
        for copy in copies:
            copy.wait()

    return pl.pallas_call(
        kernel,
        in_specs=[pl.BlockSpec(memory_space=pltpu.VMEM), pl.BlockSpec(memory_space=pl.ANY)],
        out_specs=pl.BlockSpec(memory_space=pl.ANY),
        out_shape=pltpu.HBM((NYH * half, cols), BF16),
        scratch_shapes=[pltpu.VMEM((NYH * half, cols), BF16), pltpu.SemaphoreType.DMA((NYH,))],
        compiler_params=pltpu.CompilerParams(vmem_limit_bytes=8 * MIB),
    )(inside(pieces), after)


def project(at, got, hidden, w, w_other, factor, after):
    rows, cols = w.shape
    toks = got.shape[0]
    steps = 4
    wide = cols // steps

    def kernel(at_ref, a_ref, b_ref, c_ref, d_ref, w_ref, v_ref, after_ref, far_ref, near_ref):
        far_ref[...] = ((dot(a_ref[...], w_ref[...]) + dot(b_ref[...], v_ref[...])) * factor).astype(BF16)
        near_ref[...] = (dot(c_ref[...], w_ref[...]) + dot(d_ref[...], v_ref[...])) * factor

    def left(k):
        return pl.BlockSpec((toks, rows), lambda i, at: (0, at[k]))

    column = pl.BlockSpec((toks, wide), lambda i, at: (0, i))
    wspec = pl.BlockSpec((rows, wide), lambda i, at: (0, i))
    return call(
        kernel,
        (steps,),
        [left(2), left(4), left(1), left(3), wspec, wspec, pl.BlockSpec(memory_space=pl.ANY)],
        [column, column],
        [pltpu.HBM((toks, cols), BF16), jax.ShapeDtypeStruct((toks, cols), F32)],
        8 * toks * rows * cols,
        4 * rows * cols + 8 * toks * rows,
        at,
        got,
        got,
        outside(hidden),
        outside(hidden),
        outside(w),
        outside(w_other),
        after,
    )


def hold(array, *after):
    hbm = pl.BlockSpec(memory_space=pl.ANY)
    small = (8, 128)

    def kernel(*refs):
        refs[-1][...] = jnp.zeros(small, F32)

    return pl.pallas_call(
        kernel,
        in_specs=[hbm] * (1 + len(after)),
        out_specs=[hbm, pl.BlockSpec(memory_space=pltpu.VMEM)],
        out_shape=[
            jax.ShapeDtypeStruct(array.shape, array.dtype),
            jax.ShapeDtypeStruct(small, F32),
        ],
        input_output_aliases={0: 0},
        compiler_params=pltpu.CompilerParams(vmem_limit_bytes=MIB),
    )(array, *after)


def finish(near, far):
    def kernel(n_ref, f_ref, o_ref):
        o_ref[...] = (n_ref[...] + f_ref[...].astype(F32)).astype(BF16)

    vmem = pl.BlockSpec(memory_space=pltpu.VMEM)
    return pl.pallas_call(
        kernel,
        in_specs=[vmem, vmem],
        out_specs=vmem,
        out_shape=jax.ShapeDtypeStruct(near.shape, BF16),
        compiler_params=pltpu.CompilerParams(vmem_limit_bytes=16 * MIB),
    )(near, far)


def inner_step(at, hidden, near, far_got, far, upstreams, w, m1, m2, factor):
    rows, cols = w.shape
    toks = hidden.shape[0]
    tall = 384
    steps = rows // tall

    def kernel(at_ref, h_ref, n_ref, g_ref, f_ref, hu_ref, nu_ref, gu_ref, fu_ref, w_ref, m1_ref, m2_ref, o_ref):
        gradient = dot_t(h_ref[...], hu_ref[...]) + dot_t(n_ref[...], nu_ref[...])
        gradient = gradient + dot_t(g_ref[...], gu_ref[...]) + dot_t(f_ref[...], fu_ref[...])
        gradient = gradient * factor
        moment_new = beta_one * m1_ref[...].astype(F32) + (1.0 - beta_one) * gradient
        second_new = beta_two * m2_ref[...].astype(F32) + (1.0 - beta_two) * gradient * gradient
        scale = jnp.sqrt(second_new * (1.0 / bias_two)) + epsilon
        stepped = moment_new * (mixing * inner_rate / bias_one) / scale
        half = (mixing * (1.0 - inner_rate * decay_rate)) * w_ref[...].astype(F32) - stepped
        o_ref[...] = half.astype(BF16)

    def left(first):
        return pl.BlockSpec((toks, tall), first)

    whole = pl.BlockSpec((toks, cols), lambda i, at: (0, 0))
    own = pl.BlockSpec((tall, cols), lambda i, at: (i, 0))
    spec = pltpu.PrefetchScalarGridSpec(
        num_scalar_prefetch=1,
        grid=(steps,),
        in_specs=[
            left(lambda i, at: (0, at[1] * steps + i)),
            left(lambda i, at: (0, i)),
            left(lambda i, at: (0, at[2] * steps + i)),
            left(lambda i, at: (0, i)),
            whole,
            whole,
            whole,
            whole,
            own,
            own,
            own,
        ],
        out_specs=own,
    )
    operands = [outside(hidden), near, far_got, far] + upstreams + [outside(w), outside(m1), outside(m2)]
    return pl.pallas_call(
        kernel,
        grid_spec=spec,
        out_shape=pltpu.HBM((rows, cols), BF16),
        compiler_params=pltpu.CompilerParams(vmem_limit_bytes=40 * MIB),
        cost_estimate=pl.CostEstimate(
            flops=8 * toks * rows * cols, bytes_accessed=10 * rows * cols, transcendentals=0
        ),
    )(at, *operands)


def merge(at, kept, spread):
    rows, cols = kept.shape
    block = rows // NX

    def kernel(at_ref, k_ref, a_ref, b_ref, c_ref, d_ref, o_ref, kept_ref, held, in_sems, out_sems):
        refs = [a_ref, b_ref, c_ref, d_ref]
        places = [pl.ds(pl.multiple_of(lax.rem(at_ref[0] + NX - d, NX) * block, 16), block) for d in range(NX)]
        ins = [pltpu.make_async_copy(k_ref.at[places[d]], kept_ref.at[d], in_sems.at[d]) for d in range(NX)]
        outs = [pltpu.make_async_copy(held.at[d], o_ref.at[places[d]], out_sems.at[d]) for d in range(NX)]
        for copy in ins:
            copy.start()
        for d in range(NX):
            ins[d].wait()
            new = (1.0 - mixing) * refs[d][...].astype(F32)
            held[d] = (kept_ref[d].astype(F32) + new).astype(BF16)
            outs[d].start()
        for copy in outs:
            copy.wait()

    vmem, hbm = pl.BlockSpec(memory_space=pltpu.VMEM), pl.BlockSpec(memory_space=pl.ANY)
    return pl.pallas_call(
        kernel,
        in_specs=[pl.BlockSpec(memory_space=pltpu.SMEM), hbm] + [vmem] * NX,
        out_specs=hbm,
        out_shape=jax.ShapeDtypeStruct((rows, cols), BF16),
        scratch_shapes=[
            pltpu.VMEM((NX, block, cols), BF16),
            pltpu.VMEM((NX, block, cols), BF16),
            pltpu.SemaphoreType.DMA((NX,)),
            pltpu.SemaphoreType.DMA((NX,)),
        ],
        compiler_params=pltpu.CompilerParams(vmem_limit_bytes=24 * MIB),
        cost_estimate=pl.CostEstimate(flops=2 * rows * cols, bytes_accessed=8 * rows * cols, transcendentals=0),
    )(at, outside(kept), *[inside(x) for x in spread])


def on_device(hidden, upstream, weights, moment_one, moment_two, global_params, outer_momentum):
    width = hidden.shape[2]
    rows = weights.shape[1]
    factor = float(width) ** (-0.5)
    own = global_params.shape[1]
    block = rows // NX
    rep, fsdp = lax.axis_index("rep"), lax.axis_index("fsdp")
    core, pair = fsdp % NC, fsdp // NC
    x_at = rep // PLANE
    sibling = pair * NC + 1 - core
    at = jnp.stack([x_at, fsdp, core, sibling, 1 - core, pair]).astype(jnp.int32)
    w, h, u = weights[0], hidden[0], upstream[0]

    *sent, h_sent = cut(at, w, h)
    got = [swap(x, TO_X[d]) for d, x in enumerate(sent, 1)]

    w_other = swap(w, TO_OTHER_CORE)
    h_got = swap(h_sent, TO_OTHER_CHIP)
    h_near = swap(lax.dynamic_slice_in_dim(h, sibling * rows, rows, 1), TO_OTHER_CORE)
    u_near = swap(u, TO_OTHER_CORE)
    h_far = swap(lax.dynamic_slice_in_dim(h_got, (1 - core) * rows, rows, 1), TO_OTHER_CORE)

    mine = lax.dynamic_slice_in_dim(w, x_at * block, block, 0)
    sum_x = sum_over_x([mine] + got, own, h_got)
    parts = over(sum_x, BACK_GROUPS)
    far_sent, near = project(at, h_got, h, w, w_other, factor, sum_x)
    u_got, token = hold(swap(u, TO_OTHER_CHIP), far_sent)
    u_far = swap(u_got, TO_OTHER_CORE)
    renewed, new_global, new_momentum = outer_step(
        parts, global_params[0], outer_momentum[0], lax.axis_size("rep"), token
    )
    corners = jnp.stack([x[:8, :128] for x in (u_far, h_far)])
    spread = [pack(over(renewed, HZ_GROUPS), own, corners)]
    for d in range(1, NX):
        spread.append(swap(spread[0], TO_X[d]))

    upstreams = [u, u_near, u_got, u_far]
    kept = inner_step(at, h, h_near, h_got, h_far, upstreams, w, moment_one[0], moment_two[0], factor)
    values = finish(near, swap(far_sent, TO_OTHER_CHIP))
    merged = merge(at, kept, spread)
    return (values[None], merged[None], new_global[None], new_momentum[None])


def solution(mesh):
    return jax.shard_map(
        on_device,
        mesh=mesh,
        in_specs=(
            P("rep", "fsdp", None),
            P("rep", "fsdp", None),
            P("rep", "fsdp", None),
            P("rep", "fsdp", None),
            P("rep", "fsdp", None),
            P("fsdp", "rep", None),
            P("fsdp", "rep", None),
        ),
        out_specs=(
            P("rep", "fsdp", None),
            P("rep", "fsdp", None),
            P("fsdp", "rep", None),
            P("fsdp", "rep", None),
        ),
        check_vma=False,
    )
```
